32 devices in a mesh: dp: 2 (over x), pipe: 4 (over z), tensor: 4 (over y, core).
Axes of the slice: x: 2, y: 2, z: 4, core: 2. Of those that a mesh axis runs over, the one named last changes fastest.
Arguments:
- inputs: bfloat16 [4, 3072, 8192], P('pipe', 'dp', 'tensor'), may hold values from -6 to 6
- upstream: bfloat16 [4, 3072, 8192], P('pipe', 'dp', 'tensor'), may hold values from -6 to 6
- factor_one: bfloat16 [4, 32, 4, 256, 256], P('pipe', 'tensor'), may hold values from -0.375 to 0.375
- factor_two: bfloat16 [4, 128, 256, 256], P('pipe', 'tensor'), may hold values from -0.375 to 0.375
- factor_three: bfloat16 [4, 128, 256, 256], P('pipe', 'tensor'), may hold values from -0.375 to 0.375
- factor_four: bfloat16 [4, 32, 4, 256, 256], P('pipe', 'tensor'), may hold values from -0.1875 to 0.1875
Outputs:
- y_next: bfloat16 [4, 3072, 8192], P('pipe', 'dp', 'tensor')
- dx_prev: bfloat16 [4, 3072, 8192], P('pipe', 'dp', 'tensor')
- grad_one: float32 [4, 32, 4, 256, 256], P('pipe', 'tensor')
- grad_two: float32 [4, 128, 256, 256], P('pipe', 'tensor')
- grad_three: float32 [4, 128, 256, 256], P('pipe', 'tensor')
- grad_four: float32 [4, 32, 4, 256, 256], P('pipe', 'tensor')
The draws below stay inside these ranges and needn't reach their ends.
All inputs are finite; a program needn't handle non-finite values.
Results may differ from the reference program's by a relative error of at most 0.0068.
Values may be sent and summed in bfloat16 or wider, within the bound.
A program may use at most 384 MiB of HBM per device.

```python
import jax
import jax.numpy as jnp
from jax import lax

D = 8192
BS = 256
SECTIONS = 4
TOKENS = 3072
NG = 32
NM = 128
EXPAND = 4


def steps_of(key, extent, split, smallest, top_value):
    def one(axis_at, blocks):
        draws = jax.random.uniform(jax.random.fold_in(jax.random.fold_in(key, 6), axis_at), (blocks,), jnp.float32, smallest / len(split), top_value / len(split))
        return jnp.repeat(jnp.exp(draws), extent[axis_at] // blocks).reshape((-1,) + (1,) * (len(extent) - axis_at - 1))

    factor_of = one(*split[0])
    for cut in split[1:]:
        factor_of = factor_of * one(*cut)
    return factor_of


def normal_values(own_key, dims, scale, most, shards=(), held_as=jnp.bfloat16):
    entries = jax.random.normal(own_key, dims, jnp.float32) * scale
    if len(shards) > 0:
        entries = steps_of(own_key, dims, shards, -0.22, 0.18) * entries
    return jnp.clip(entries, min=-most, max=most).astype(held_as)


def setup_inputs(seed: int = 0) -> dict:
    arg_keys = jax.random.split(jax.random.key(seed), 7)
    inputs = normal_values(arg_keys[0], (SECTIONS, TOKENS, D), 1.0, 6.0, ((0, 4), (1, 2), (2, 4)))
    upstream = normal_values(arg_keys[1], (SECTIONS, TOKENS, D), 1.0, 6.0, ((0, 4), (1, 2), (2, 4)))
    factor_one = normal_values(arg_keys[2], (SECTIONS, NG, EXPAND, BS, BS), BS ** -0.5, 0.375, ((0, 4), (1, 4)))
    factor_two = normal_values(arg_keys[3], (SECTIONS, NM, BS, BS), BS ** -0.5, 0.375, ((0, 4), (1, 4)))
    factor_three = normal_values(arg_keys[4], (SECTIONS, NM, BS, BS), BS ** -0.5, 0.375, ((0, 4), (1, 4)))
    factor_four = normal_values(arg_keys[5], (SECTIONS, NG, EXPAND, BS, BS), (EXPAND * BS) ** -0.5, 0.1875, ((0, 4), (1, 4)))
    return {"inputs": inputs, "upstream": upstream, "factor_one": factor_one, "factor_two": factor_two, "factor_three": factor_three, "factor_four": factor_four}


def permute(blocks):
    rows, count, width = blocks.shape
    inner = width // count
    return blocks.reshape(rows, count, count, inner).transpose(0, 2, 1, 3).reshape(rows, count, width)

def one_section(operands):
    acts, grad_out, factor_one, factor_two, factor_three, factor_four = operands
    groups, expand, bsize = (factor_one.shape[0], factor_one.shape[1], factor_one.shape[2])
    rows = acts.shape[0]
    one_f = factor_one.astype(jnp.float32)
    two_f = factor_two.astype(jnp.float32)
    three_f = factor_three.astype(jnp.float32)
    four_f = factor_four.astype(jnp.float32)
    grouped = acts.reshape(rows, groups, bsize).astype(jnp.float32)
    lifted = jnp.einsum('tgi,gkij->tgkj', grouped, one_f).astype(jnp.bfloat16).reshape(rows, groups * expand, bsize)
    mixed = permute(lifted)
    preact = jnp.einsum('tcj,cjn->tcn', mixed.astype(jnp.float32), two_f)
    active = jax.nn.gelu(preact).astype(jnp.bfloat16)
    narrowed = jnp.einsum('tcn,cno->tco', active.astype(jnp.float32), three_f).astype(jnp.bfloat16)
    spread = permute(narrowed)
    spread_four = spread.reshape(rows, groups, expand, bsize).astype(jnp.float32)
    output = jnp.einsum('tgkr,gkro->tgo', spread_four, four_f).astype(jnp.bfloat16).reshape(rows, groups * bsize)
    grad_grouped = grad_out.reshape(rows, groups, bsize).astype(jnp.float32)
    grad_spread = jnp.einsum('tgo,gkro->tgkr', grad_grouped, four_f).astype(jnp.bfloat16).reshape(rows, groups * expand, bsize)
    grad_four = jnp.einsum('tgkr,tgo->gkro', spread_four, grad_grouped)
    grad_narrow = permute(grad_spread)
    grad_active = jnp.einsum('tco,cno->tcn', grad_narrow.astype(jnp.float32), three_f)
    grad_three = jnp.einsum('tcn,tco->cno', active.astype(jnp.float32), grad_narrow.astype(jnp.float32))
    pulled = jax.vjp(jax.nn.gelu, preact)[1]
    grad_pre = pulled(grad_active)[0].astype(jnp.bfloat16)
    grad_two = jnp.einsum('tcj,tcn->cjn', mixed.astype(jnp.float32), grad_pre.astype(jnp.float32))
    grad_mixed = jnp.einsum('tcn,cjn->tcj', grad_pre.astype(jnp.float32), two_f).astype(jnp.bfloat16)
    grad_lift = permute(grad_mixed)
    lift_four = grad_lift.reshape(rows, groups, expand, bsize).astype(jnp.float32)
    grad_input = jnp.einsum('tgkj,gkij->tgi', lift_four, one_f).astype(jnp.bfloat16).reshape(rows, groups * bsize)
    grad_one = jnp.einsum('tgi,tgkj->gkij', grouped, lift_four)
    return (output, grad_input, grad_one, grad_two, grad_three, grad_four)

def reference(inputs, upstream, factor_one, factor_two, factor_three, factor_four):
    output, grad_input, grad_one, grad_two, grad_three, grad_four = lax.map(one_section, (inputs, upstream, factor_one, factor_two, factor_three, factor_four))
    y_next = jnp.concatenate([jnp.zeros_like(output[:1]), output[:-1]], axis=0)
    dx_prev = jnp.concatenate([grad_input[1:], jnp.zeros_like(grad_input[:1])], axis=0)
    return (y_next, dx_prev, grad_one, grad_two, grad_three, grad_four)
```

```python
import functools
import math

import jax
import jax.numpy as jnp
from jax import lax
from jax.experimental import pallas as pl
from jax.experimental.pallas import tpu as pltpu
from jax.sharding import PartitionSpec as P

F32, BF16 = jnp.float32, jnp.bfloat16
HALVES = 2
ROOT = math.sqrt(2.0 / math.pi)
CUBE = 0.044715
VMEM = 48 * 2**20


def params():
    return pltpu.CompilerParams(vmem_limit_bytes=VMEM)


def contract(a, b, da, db):
    return lax.dot_general(a, b, (((da,), (db,)), ((), ())), preferred_element_type=F32)


def exchange(value, axis, mask):
    count = lax.axis_size(axis)
    return lax.ppermute(value, axis, [(i, i ^ mask) for i in range(count)])


def shifted(value, axis, steps):
    count = lax.axis_size(axis)
    leading, last = (max(0, -steps), min(count, count - steps))
    return lax.ppermute(value, axis, [(source, source + steps) for source in range(leading, last)])


def lift_kernel(spot, x_ref, w_ref, *refs):
    out_ref = refs[-1]
    local = out_ref.shape[0]
    bsize = w_ref.shape[2]
    parts = []
    for j in range(2):
        block = contract(w_ref[j], x_ref[:, j * bsize:(j + 1) * bsize], 1, 1)
        parts.append(block.reshape(local, block.shape[0] // local, block.shape[1]))
    out_ref[...] = jnp.concatenate(parts, axis=1).astype(BF16)


def lift(spot, x, w, buffer, local, width):
    groups, rows, bsize = w.shape
    tokens = x.shape[0]
    pairs = groups // 2
    in_specs = [
        pl.BlockSpec((tokens, 2 * bsize), lambda i, s: (0, i)),
        pl.BlockSpec((2, rows, bsize), lambda i, s: (i, 0, 0)),
    ]
    args = [x, w]
    aliases = {}
    if buffer is not None:
        in_specs.append(pl.BlockSpec(memory_space=pl.ANY))
        args.append(buffer)
        aliases = {3: 0}
    high = 2 * rows // local
    return pl.pallas_call(
        lift_kernel,
        grid_spec=pltpu.PrefetchScalarGridSpec(
            num_scalar_prefetch=1,
            grid=(pairs,),
            in_specs=in_specs,
            out_specs=pl.BlockSpec((local, high, tokens), lambda i, s: (0, s[0] * pairs + i, 0)),
        ),
        out_shape=jax.ShapeDtypeStruct((local, width, tokens), BF16),
        input_output_aliases=aliases,
        compiler_params=params(),
        cost_estimate=pl.CostEstimate(
            flops=2 * groups * rows * bsize * tokens,
            bytes_accessed=2 * (groups * bsize * tokens + w.size + groups * rows * tokens),
            transcendentals=0,
        ),
        name="lift",
    )(spot, *args)


def middle_kernel(adds, mixed_ref, gn_ref, two_ref, three_ref, *refs):
    if adds:
        old_two, old_three, narrow_ref, gm_ref, g2_ref, g3_ref = refs
    else:
        narrow_ref, gm_ref, g2_ref, g3_ref = refs
    mixed, gn, two, three = mixed_ref[0], gn_ref[0], two_ref[0], three_ref[0]
    pre = contract(two, mixed, 0, 0)
    grad_active = contract(three, gn, 1, 0)
    square = pre * pre
    tanh = jnp.tanh(pre * (ROOT + (ROOT * CUBE) * square))
    half = 0.5 + 0.5 * tanh
    active = (pre * half).astype(BF16)
    slope = half + (0.5 * pre) * (1.0 - tanh * tanh) * (ROOT + (3.0 * ROOT * CUBE) * square)
    grad_pre = (grad_active * slope).astype(BF16)
    narrow_ref[0] = contract(three, active, 0, 0).astype(BF16)
    gm_ref[0] = contract(two, grad_pre, 1, 0).astype(BF16)
    g3 = contract(active, gn, 1, 1)
    g2 = contract(mixed, grad_pre, 1, 1)
    if adds:
        g3 = g3 + old_three[0]
        g2 = g2 + old_two[0]
    g2_ref[0] = g2
    g3_ref[0] = g3


def middle(mixed, gn, two, three, olds):
    local, width, tokens = mixed.shape
    data = pl.BlockSpec((1, width, tokens), lambda c: (c, 0, 0))
    factor = pl.BlockSpec((1, width, width), lambda c: (c, 0, 0))
    grads = jax.ShapeDtypeStruct((local, width, width), F32)
    hidden = jax.ShapeDtypeStruct(mixed.shape, BF16)
    return pl.pallas_call(
        functools.partial(middle_kernel, bool(olds)),
        grid=(local,),
        in_specs=[data, data, factor, factor] + [factor] * len(olds),
        out_specs=[data, data, factor, factor],
        out_shape=[hidden, hidden, grads, grads],
        compiler_params=params(),
        cost_estimate=pl.CostEstimate(
            flops=12 * local * width * width * tokens,
            bytes_accessed=8 * local * width * tokens + 12 * local * width * width,
            transcendentals=local * width * tokens,
        ),
        name="middle",
    )(mixed, gn, two, three, *olds)


def last_kernel(adds, olds, spot, narrow_ref, gm_ref, one_ref, four_ref, x_ref, up_ref, *refs):
    refs = list(refs)
    added = [refs.pop(0) for _ in range(2)] if adds else None
    kept = [refs.pop(0) for _ in range(2)] if olds else None
    out_ref, gi_ref, g1_ref, g4_ref = refs
    bsize = one_ref.shape[2]
    rows = one_ref.shape[1]
    local, high, tokens = narrow_ref.shape
    low = high // 2
    narrow = narrow_ref[...].astype(F32)
    lifted = gm_ref[...].astype(F32)
    for j in range(2):
        cols = slice(j * bsize, (j + 1) * bsize)
        spread = narrow[:, j * low:(j + 1) * low].reshape(rows, tokens).astype(BF16)
        grad_lift = lifted[:, j * low:(j + 1) * low].reshape(rows, tokens).astype(BF16)
        out = contract(spread, four_ref[j], 0, 0)
        gi = contract(grad_lift, one_ref[j], 0, 0)
        if adds:
            out = out + added[0][:, cols].astype(F32)
            gi = gi + added[1][:, cols].astype(F32)
        out_ref[:, cols] = out.astype(BF16)
        gi_ref[:, cols] = gi.astype(BF16)
        g1 = contract(grad_lift, x_ref[:, cols], 1, 0)
        g4 = contract(spread, up_ref[:, cols], 1, 0)
        if olds:
            g1 = g1 + kept[0][j]
            g4 = g4 + kept[1][j]
        g1_ref[j] = g1
        g4_ref[j] = g4


def last(spot, narrow, gm, one, four, x, up, added, olds):
    local, width, tokens = narrow.shape
    groups, rows, bsize = one.shape
    pairs = groups // 2
    high = 2 * rows // local
    hidden = pl.BlockSpec((local, high, tokens), lambda i, s: (0, s[0] * pairs + i, 0))
    factor = pl.BlockSpec((2, rows, bsize), lambda i, s: (i, 0, 0))
    data = pl.BlockSpec((tokens, 2 * bsize), lambda i, s: (0, i))
    return pl.pallas_call(
        functools.partial(last_kernel, bool(added), bool(olds)),
        grid_spec=pltpu.PrefetchScalarGridSpec(
            num_scalar_prefetch=1,
            grid=(pairs,),
            in_specs=[hidden, hidden, factor, factor, data, data]
            + [data] * len(added) + [factor] * len(olds),
            out_specs=[data, data, factor, factor],
        ),
        out_shape=[
            jax.ShapeDtypeStruct(x.shape, BF16),
            jax.ShapeDtypeStruct(x.shape, BF16),
            jax.ShapeDtypeStruct(one.shape, F32),
            jax.ShapeDtypeStruct(one.shape, F32),
        ],
        compiler_params=params(),
        cost_estimate=pl.CostEstimate(
            flops=8 * groups * rows * bsize * tokens,
            bytes_accessed=4 * groups * rows * tokens + 8 * x.size + 12 * one.size,
            transcendentals=0,
        ),
        name="last",
    )(spot, narrow, gm, one, four, x, up, *added, *olds)


def gather(value, bits):
    held = {0: value}
    for bit in reversed(bits):
        for q in list(held):
            held[q ^ bit] = exchange(held[q], "tensor", bit)
    return held


def shards(inputs, upstream, factor_one, factor_two, factor_three, factor_four):
    parts = lax.axis_size("tensor")
    bits = [1 << b for b in range(parts.bit_length() - 1)]
    me = lax.axis_index("tensor")
    acts, grad_out = inputs[0], upstream[0]
    first, second, third, fourth = factor_one[0], factor_two[0], factor_three[0], factor_four[0]
    groups, expand, bsize = first.shape[:3]
    local = second.shape[0]
    inner = bsize // (parts * local)
    rows = local * expand * inner
    tokens = acts.shape[0] // HALVES
    spots = {q: (me ^ q).astype(jnp.int32).reshape(1) for q in range(parts)}

    ones = first.reshape(groups, expand, bsize, parts, local, inner).transpose(3, 0, 4, 1, 5, 2)
    ones = ones.reshape(parts, groups, rows, bsize)
    fours = fourth.reshape(groups, expand, parts, local, inner, bsize).transpose(2, 0, 3, 1, 4, 5)
    fours = fours.reshape(parts, groups, rows, bsize)
    one, four = {}, {}
    for q in reversed(range(parts)):
        pair = jnp.stack([
            lax.dynamic_index_in_dim(ones, me ^ q, 0, False),
            lax.dynamic_index_in_dim(fours, me ^ q, 0, False),
        ])
        if q:
            pair = exchange(pair, "tensor", q)
        one[q], four[q] = pair[0], pair[1]

    grads_mid, grads_end = (), {q: () for q in range(parts)}
    y_parts, dx_parts = [], []
    gathered = []
    for h in range(HALVES):
        rows_h = slice(h * tokens, (h + 1) * tokens)
        gathered.append((gather(acts[rows_h], bits), gather(grad_out[rows_h], bits)))
    for h in range(HALVES):
        xs, ups = gathered[h]
        mixed = grad_narrow = None
        for q in xs:
            mixed = lift(spots[q], xs[q], one[q], mixed, local, bsize)
            grad_narrow = lift(spots[q], ups[q], four[q], grad_narrow, local, bsize)
        narrow, grad_mixed, g2, g3 = middle(mixed, grad_narrow, second, third, grads_mid)
        grads_mid = (g2, g3)
        totals = {}
        for q in sorted(range(parts), key=lambda q: (-(q & -2), -(q & 1))):
            added = ()
            if not q & 1:
                added = tuple(exchange(t, "tensor", 1) for t in totals.pop(q ^ 1))
            out, gi, g1, g4 = last(
                spots[q], narrow, grad_mixed, one[q], four[q], xs[q], ups[q], added, grads_end[q]
            )
            grads_end[q] = (g1, g4)
            totals[q] = (out, gi)
        for bit in bits[1:]:
            for q in [q for q in totals if q & bit]:
                came = [exchange(t, "tensor", bit) for t in totals.pop(q)]
                totals[q ^ bit] = tuple(
                    (t.astype(F32) + c.astype(F32)).astype(BF16)
                    for t, c in zip(totals[q ^ bit], came)
                )
        out, gi = totals[0]
        y_parts.append(shifted(out, "pipe", 1))
        dx_parts.append(shifted(gi, "pipe", -1))
    y_next = jnp.concatenate(y_parts, axis=0)[None]
    dx_prev = jnp.concatenate(dx_parts, axis=0)[None]

    mids = []
    for grad in grads_mid:
        mine = grad.astype(BF16)
        other = exchange(mine, "dp", 1)
        mids.append((mine.astype(F32) + other.astype(F32))[None])

    split = lax.axis_index("dp")
    cut = groups // 2
    own = []
    for q in range(parts):
        both = jnp.stack(grads_end[q])
        keep = lax.dynamic_slice_in_dim(both, split * cut, cut, 1)
        give = lax.dynamic_slice_in_dim(both, (1 - split) * cut, cut, 1).astype(BF16)
        total = (keep + exchange(give, "dp", 1).astype(F32)).astype(BF16)
        own.append(exchange(total, "tensor", q) if q else total)
    stacked = jnp.stack(own)
    other = exchange(stacked, "dp", 1)
    low = jnp.where(split == 0, stacked, other)
    high = jnp.where(split == 0, other, stacked)
    whole = jnp.concatenate([low, high], axis=2)
    whole = jnp.stack([lax.dynamic_index_in_dim(whole, me ^ p, 0, False) for p in range(parts)])
    whole = whole.reshape(parts, 2, groups, local, expand, inner, bsize)
    grad_one = whole[:, 0].transpose(1, 3, 5, 0, 2, 4).reshape(first.shape).astype(F32)
    grad_four = whole[:, 1].transpose(1, 3, 0, 2, 4, 5).reshape(fourth.shape).astype(F32)
    return (y_next, dx_prev, grad_one[None], mids[0], mids[1], grad_four[None])


def solution(mesh):
    specs = (
        P("pipe", "dp", "tensor"),
        P("pipe", "dp", "tensor"),
        P("pipe", "tensor", None, None, None),
        P("pipe", "tensor", None, None),
        P("pipe", "tensor", None, None),
        P("pipe", "tensor", None, None, None),
    )
    return jax.shard_map(shards, mesh=mesh, in_specs=specs, out_specs=specs, check_vma=False)
```
